32 devices in a mesh: grp: 4 (over y, x), sub: 8 (over z, core).
Axes of the slice: x: 2, y: 2, z: 4, core: 2. Of those that a mesh axis runs over, the one named last changes fastest.
Arguments:
- solution: float32 [4, 8, 16, 512], P('grp', 'sub'), may hold values from -6 to 6
- residual: float32 [4, 8, 16, 512], P('grp', 'sub'), as said below
- direction: float32 [4, 8, 16, 512], P('grp', 'sub'), as said below
- inner_old: float32 [16], replicated, may hold values from 0.5 to 2
- interior: bfloat16 [4, 8, 16, 1536], P('grp', 'sub'), may hold values from -6 to 6
- weights: float32 [4, 8, 512], P('grp', 'sub'), as said below
- neighbours: int32 [4, 8, 4], P('grp', 'sub'), may hold values from -1 to 7, as said below
- coarse_rows: int32 [4, 8, 12], P('grp', 'sub'), may hold values from -1 to 119, as said below
- coarse_basis_matrix: float32 [4, 8, 12, 512], P('grp', 'sub'), may hold values from -0.5 to 0.5
- local_solver: bfloat16 [4, 8, 512, 512], P('grp', 'sub'), as said below
- schur_matrix: bfloat16 [4, 8, 512, 512], P('grp', 'sub'), as said below
- extension_values: bfloat16 [4, 8, 12, 2, 128, 128], P('grp', 'sub'), may hold values from -0.375 to 0.375
- extension_block_index: int32 [4, 8, 12, 2], P('grp', 'sub'), may hold values from 0 to 3
- coarse_inverse: float32 [120, 120], P('sub'), as said below
Outputs:
- solution_new: float32 [4, 8, 16, 512], P('grp', 'sub')
- residual_new: float32 [4, 8, 16, 512], P('grp', 'sub')
- direction_new: float32 [4, 8, 16, 512], P('grp', 'sub')
- interior_new: bfloat16 [4, 8, 16, 1536], P('grp', 'sub')
- inner_new: float32 [16], replicated
The draws below stay inside these ranges and needn't reach their ends.
Inputs may be any that keep to these rules, and one draw needn't show every extreme that they name: Within a group the relation is symmetric: if neighbours[g, s, k] = t >= 0 then neighbours[g, t, k XOR 1] = s; the neighbours of one subdomain are distinct; -1 marks an absent block. `coarse_rows`: both subdomains of a shared face block list the same 3 rows for it, each coarse row is named by exactly two entries, and absent blocks hold -1. On a shared face the two sides' weights add up to 1; absent blocks hold 0. `residual`: equal on the two sides of every shared face, 0 on absent blocks. `direction`: equal on the two sides of every shared face, 0 on absent blocks. `local_solver`: Symmetric, with a positive diagonal larger than the sum of the magnitudes of its row's other entries. `schur_matrix`: Symmetric, with a positive diagonal larger than the sum of the magnitudes of its row's other entries. `coarse_inverse`: symmetric positive definite.
All inputs are finite; a program needn't handle non-finite values.
Results may differ from the reference program's by a relative error of at most 0.0019.
The reference program's roundings to bfloat16 on the way count: a program that leaves them out, or rounds other values in their place, can miss the bound.
Values sent between devices are 32-bit elements; how exact they have to be, the bound alone decides.
A program may use at most 64 MiB of HBM per device.

```python
import math
import jax
import jax.numpy as jnp
from jax import lax

FACES_PER_BLOCK = 128
SLOT_TOTAL = 4
PRIMAL_COUNT = 3
FEEDING_BLOCKS = 2
LOAD_CASES = 16
INTERIOR_BLOCKS = 12
GROUP_COUNT = 4
SUBDOMAIN_COUNT = 8
INTERFACE_FACES = 512
NIN = 1536
BLOCKS = 40
NCOARSE = 120


MIRROR = (1, 0, 3, 2)


def grid_layout(key):
    columns = SUBDOMAIN_COUNT // 4
    group_keys = jax.random.split(jax.random.fold_in(key, 101), GROUP_COUNT)
    placed = jax.vmap(lambda one_key: jax.random.permutation(one_key, SUBDOMAIN_COUNT))(group_keys)
    where_cell = jnp.argsort(placed, axis=1, stable=True)
    cell_row = where_cell // columns
    cell_column = where_cell % columns
    targets = jnp.stack([where_cell - 1, where_cell + 1, where_cell - columns, where_cell + columns], axis=-1)
    allowed = jnp.stack([cell_column > 0, cell_column < columns - 1, cell_row > 0, cell_row < 3], axis=-1)
    clipped = jnp.clip(targets, 0, SUBDOMAIN_COUNT - 1)
    found = jax.vmap(lambda group_rows, group_index: group_rows[group_index])(placed, clipped)
    neighbour = jnp.where(allowed, found, -1).astype(jnp.int32)
    flat_count = 4 * (columns - 1)
    local_ids = jnp.stack([cell_row * (columns - 1) + cell_column - 1, cell_row * (columns - 1) + cell_column, flat_count + (cell_row - 1) * columns + cell_column, flat_count + cell_row * columns + cell_column], axis=-1)
    group_ids = jnp.arange(GROUP_COUNT, dtype=jnp.int32)[:, None, None] * (7 * columns - 4)
    global_ids = jnp.clip(local_ids + group_ids, 0, BLOCKS - 1)
    shuffled = jax.random.permutation(jax.random.fold_in(key, 102), BLOCKS)
    block_ids = jnp.where(allowed, shuffled[global_ids], -1).astype(jnp.int32)
    return (neighbour, block_ids)


def partner_draw(blocked, neighbour):
    clipped = jnp.maximum(neighbour, 0)
    active = (neighbour >= 0).astype(jnp.float32)
    pieces = []
    for neighbour_slot_index in range(SLOT_TOTAL):
        source = blocked[:, :, :, MIRROR[neighbour_slot_index], :]
        taken = jax.vmap(lambda group_rows, group_index: group_rows[group_index])(source, clipped[:, :, neighbour_slot_index])
        pieces.append(taken * active[:, :, neighbour_slot_index][:, :, None, None])
    return jnp.stack(pieces, axis=3)


def draw_neighbours(key, part):
    neighbour, block_ids = grid_layout(key)
    return neighbour


def draw_coarse_rows(key, part):
    neighbour, block_ids = grid_layout(key)
    offsets = jnp.arange(PRIMAL_COUNT, dtype=jnp.int32)
    full_row_count = jnp.where(block_ids[:, :, :, None] >= 0, block_ids[:, :, :, None] * PRIMAL_COUNT + offsets, -1)
    return full_row_count.reshape(GROUP_COUNT, SUBDOMAIN_COUNT, SLOT_TOTAL * PRIMAL_COUNT).astype(jnp.int32)


def draw_weights(key, part):
    neighbour, block_ids = grid_layout(key)
    active = (neighbour >= 0).astype(jnp.float32)
    stiffness_matrix = jnp.exp(jax.random.uniform(jax.random.fold_in(key, 103), (GROUP_COUNT, SUBDOMAIN_COUNT, 1, SLOT_TOTAL, FACES_PER_BLOCK), minval=jnp.log(0.1), maxval=jnp.log(10.0)))
    other = partner_draw(stiffness_matrix, neighbour)
    ratio = stiffness_matrix / (stiffness_matrix + other) * active[:, :, None, :, None]
    return ratio.reshape(GROUP_COUNT, SUBDOMAIN_COUNT, INTERFACE_FACES).astype(jnp.float32)


def consistent_field(key, salt):
    neighbour, block_ids = grid_layout(key)
    active = (neighbour >= 0).astype(jnp.float32)
    field_random_key = jax.random.fold_in(key, salt)
    base_offset = jax.random.normal(field_random_key, (GROUP_COUNT, SUBDOMAIN_COUNT, LOAD_CASES, SLOT_TOTAL, FACES_PER_BLOCK))
    summed = (base_offset + partner_draw(base_offset, neighbour)) * 0.7071 * active[:, :, None, :, None]
    return summed.reshape(GROUP_COUNT, SUBDOMAIN_COUNT, LOAD_CASES, INTERFACE_FACES).astype(jnp.float32)


def draw_residual(key, part):
    return consistent_field(key, 104)


def draw_direction(key, part):
    return consistent_field(key, 105)


def dominant(key, count, batch):
    entries = jax.random.uniform(key, batch + (count, count), minval=-1.0, maxval=1.0)
    mirrored = (entries + jnp.swapaxes(entries, -1, -2)) * (0.45 / count)
    diagonal = jnp.exp(jax.random.uniform(jax.random.fold_in(key, 7), batch + (count, 1), minval=0.0, maxval=jnp.log(2.0)))
    on_diagonal = jnp.arange(count)[:, None] == jnp.arange(count)[None, :]
    return jnp.where(on_diagonal, diagonal, mirrored)


def draw_local_solver(key, part):
    return dominant(jax.random.fold_in(key, 106), INTERFACE_FACES, (GROUP_COUNT, SUBDOMAIN_COUNT)).astype(jnp.bfloat16)


def draw_schur_matrix(key, part):
    return dominant(jax.random.fold_in(key, 107), INTERFACE_FACES, (GROUP_COUNT, SUBDOMAIN_COUNT)).astype(jnp.bfloat16)


def draw_coarse_inverse(key, part):
    entry_key = jax.random.fold_in(key, 108)
    entries = jnp.clip(jax.random.normal(entry_key, (NCOARSE, NCOARSE)), -3.0, 3.0)
    dense_part = (entries + entries.T) * (0.2 / jnp.sqrt(float(NCOARSE)))
    columns = jnp.arange(NCOARSE, dtype=jnp.int32)
    linked = jnp.zeros((NCOARSE, NCOARSE), jnp.float32)
    for salt in range(4):
        link_key = jax.random.fold_in(key, 110 + salt)
        target = jax.random.permutation(link_key, NCOARSE).astype(jnp.int32)
        sign_value = (jax.random.randint(jax.random.fold_in(link_key, 1), (NCOARSE,), 0, 2) * 2 - 1).astype(jnp.float32)
        magnitude = jax.random.uniform(jax.random.fold_in(link_key, 2), (NCOARSE,), minval=0.07, maxval=0.1)
        linked = linked + jnp.where(columns[None, :] == target[:, None], (sign_value * magnitude)[:, None], 0.0)
    mirrored = dense_part + linked + linked.T
    diagonal = jnp.exp(jax.random.uniform(jax.random.fold_in(key, 109), (NCOARSE, 1), minval=jnp.log(1.5), maxval=jnp.log(3.0)))
    on_diagonal = columns[:, None] == columns[None, :]
    return jnp.where(on_diagonal, diagonal, mirrored).astype(jnp.float32)


def plant(values, key, least, high):
    longest = values.shape.index(max(values.shape))
    spots = []
    for shift in (0, 1):
        where = [jax.random.randint(jax.random.fold_in(key, axis), (), 0, length) for axis, length in enumerate(values.shape)]
        where[longest] = (where[longest] + shift) % values.shape[longest]
        spots.append(tuple(where))
    return values.at[spots[0]].set(least).at[spots[1]].set(high)


def block_scale(rng, dims, shards, low, top_value):
    gain, own = 1.0, jax.random.fold_in(rng, 6)
    for dim, blocks in shards:
        steps = jnp.exp(jax.random.uniform(jax.random.fold_in(own, dim), (blocks,), jnp.float32, low / len(shards), top_value / len(shards)))
        gain = gain * jnp.repeat(steps, dims[dim] // blocks).reshape([-1 if axis == dim else 1 for axis in range(len(dims))])
    return gain


def centred(own_key, dims, width, reach, cuts=(), kind=jnp.bfloat16):
    gain = block_scale(own_key, dims, cuts, -0.22, 0.18) if cuts else 1.0
    result = jax.random.normal(own_key, dims, jnp.float32) * width * gain
    return jnp.minimum(jnp.maximum(result, -reach), reach).astype(kind)


def setup_inputs(seed: int = 0) -> dict:
    seeds = jax.random.split(jax.random.key(seed), 15)
    solution = centred(seeds[0], (GROUP_COUNT, SUBDOMAIN_COUNT, LOAD_CASES, INTERFACE_FACES), 1.0, 6.0, ((0, 4), (1, 8)), jnp.float32)
    residual = draw_residual(jax.random.fold_in(seeds[14], 71), 0)
    direction = draw_direction(jax.random.fold_in(seeds[14], 71), 0)
    inner_old = jnp.clip(jnp.exp(jax.random.uniform(seeds[3], (LOAD_CASES,), jnp.float32, math.log(0.5), math.log(2.0))), 0.5, 2.0)
    interior = centred(seeds[4], (GROUP_COUNT, SUBDOMAIN_COUNT, LOAD_CASES, NIN), 1.0, 6.0, ((0, 4), (1, 8)))
    weights = draw_weights(jax.random.fold_in(seeds[14], 71), 0)
    neighbours = draw_neighbours(jax.random.fold_in(seeds[14], 71), 0)
    coarse_rows = draw_coarse_rows(jax.random.fold_in(seeds[14], 71), 0)
    coarse_basis_matrix = centred(seeds[8], (GROUP_COUNT, SUBDOMAIN_COUNT, SLOT_TOTAL * PRIMAL_COUNT, INTERFACE_FACES), FACES_PER_BLOCK ** -0.5, 0.5, ((0, 4), (1, 8)), jnp.float32)
    local_solver = draw_local_solver(jax.random.fold_in(seeds[14], 71), 0)
    schur_matrix = draw_schur_matrix(jax.random.fold_in(seeds[14], 71), 0)
    extension_values = centred(seeds[11], (GROUP_COUNT, SUBDOMAIN_COUNT, INTERIOR_BLOCKS, FEEDING_BLOCKS, FACES_PER_BLOCK, FACES_PER_BLOCK), (FEEDING_BLOCKS * FACES_PER_BLOCK) ** -0.5, 0.375, ((0, 4), (1, 8)))
    extension_block_index = plant(jax.random.randint(seeds[12], (GROUP_COUNT, SUBDOMAIN_COUNT, INTERIOR_BLOCKS, FEEDING_BLOCKS), 0, SLOT_TOTAL), jax.random.fold_in(seeds[12], 1), 0, SLOT_TOTAL - 1).astype(jnp.int32)
    coarse_inverse = draw_coarse_inverse(jax.random.fold_in(seeds[14], 71), 0)
    return {"solution": solution, "residual": residual, "direction": direction, "inner_old": inner_old, "interior": interior, "weights": weights, "neighbours": neighbours, "coarse_rows": coarse_rows, "coarse_basis_matrix": coarse_basis_matrix, "local_solver": local_solver, "schur_matrix": schur_matrix, "extension_values": extension_values, "extension_block_index": extension_block_index, "coarse_inverse": coarse_inverse}


PRECISE = lax.Precision.HIGHEST
MIRROR = (1, 0, 3, 2)


def round_half(values):
    return lax.optimization_barrier(values.astype(jnp.bfloat16)).astype(jnp.float32)


def partner_field(blocked, neighbours):
    clipped = jnp.maximum(neighbours, 0)
    active = (neighbours >= 0).astype(blocked.dtype)
    pieces = []
    for neighbour_slot_index in range(SLOT_TOTAL):
        source = blocked[:, :, :, MIRROR[neighbour_slot_index], :]
        taken = jax.vmap(lambda group_rows, group_index: group_rows[group_index])(source, clipped[:, :, neighbour_slot_index])
        pieces.append(taken * active[:, :, neighbour_slot_index][:, :, None, None])
    return jnp.stack(pieces, axis=3)


def reference(solution, residual, direction, inner_old, interior, weights, neighbours, coarse_rows, coarse_basis_matrix, local_solver, schur_matrix, extension_values, extension_block_index, coarse_inverse):
    reshaped_value = (GROUP_COUNT, SUBDOMAIN_COUNT, LOAD_CASES, SLOT_TOTAL, FACES_PER_BLOCK)
    active = jnp.repeat((neighbours >= 0).astype(jnp.float32), FACES_PER_BLOCK, axis=2)[:, :, None, :]
    face_total = BLOCKS * FACES_PER_BLOCK
    scaled = weights[:, :, None, :] * residual
    local_solve = jnp.einsum("gsri,gsij->gsrj", round_half(scaled), local_solver.astype(jnp.float32), precision=PRECISE)
    coarse_part = jnp.einsum("gsri,gsmi->gsrm", scaled, coarse_basis_matrix, precision=PRECISE)
    present = (coarse_rows >= 0).astype(jnp.float32)
    clipped_rows = jnp.maximum(coarse_rows, 0)
    values = jnp.moveaxis(coarse_part * present[:, :, None, :], 2, 0).reshape(LOAD_CASES, -1)
    coarse_total = jnp.zeros((LOAD_CASES, NCOARSE), jnp.float32).at[:, clipped_rows.reshape(-1)].add(values)
    coarse_solution = jnp.dot(coarse_total, coarse_inverse, precision=PRECISE)
    coarse_local = jnp.moveaxis(coarse_solution[:, clipped_rows], 0, 2) * present[:, :, None, :]
    correction = jnp.einsum("gsrm,gsmi->gsri", coarse_local, coarse_basis_matrix, precision=PRECISE)
    weighted = weights[:, :, None, :] * (local_solve + correction)
    precond = weighted + partner_field(weighted.reshape(reshaped_value), neighbours).reshape(weighted.shape)
    inner_new = jnp.sum(residual * precond, axis=(0, 1, 3)) / (2.0 * face_total)
    direction_new = precond + (inner_new / inner_old)[None, None, :, None] * direction
    direction_half = round_half(direction_new)
    local_image = jnp.einsum("gsri,gsij->gsrj", direction_half, schur_matrix.astype(jnp.float32), precision=PRECISE)
    image_sum = active * (local_image + partner_field(local_image.reshape(reshaped_value), neighbours).reshape(local_image.shape))
    curvature = jnp.sum(direction_new * image_sum, axis=(0, 1, 3)) / (2.0 * face_total)
    step_size = inner_new / curvature
    solution_new = solution + step_size[None, None, :, None] * direction_new
    residual_new = residual - step_size[None, None, :, None] * image_sum
    direction_blocks = direction_half.reshape(reshaped_value)
    picked = jax.vmap(jax.vmap(lambda blocks_one, index_one: jnp.take(blocks_one, index_one, axis=1)))(direction_blocks, extension_block_index)
    extended = jnp.einsum("gsrbjk,gsbjkl->gsrbl", picked, extension_values.astype(jnp.float32), precision=PRECISE)
    extended = extended.reshape(GROUP_COUNT, SUBDOMAIN_COUNT, LOAD_CASES, NIN)
    interior_new = (interior.astype(jnp.float32) + step_size[None, None, :, None] * extended).astype(jnp.bfloat16)
    return (solution_new, residual_new, direction_new, interior_new, inner_new)
```

```python
import functools

import jax
import jax.numpy as jnp
from jax import lax
from jax.experimental import pallas as pl
from jax.experimental.pallas import tpu as pltpu
from jax.sharding import PartitionSpec as P

MESH = pl.DeviceIdType.MESH
LANES = 128
SUBLANES = 8
FIELD = 16
COARSE_LIMIT = 128

PRECISE = lax.Precision.HIGHEST


def contract(former, latter, former_dim, latter_dim):
    return lax.dot_general(
        former, latter, (((former_dim,), (latter_dim,)), ((), ())), precision=PRECISE
    )


def outgoing(blocks, neighbour, peer_count):
    active = (neighbour >= 0).astype(jnp.float32)
    clipped = jnp.maximum(neighbour, 0)
    outbound = jnp.transpose(blocks * active[None, :, None], (1, 0, 2))
    buffer = jnp.zeros((peer_count, blocks.shape[0], blocks.shape[2]), jnp.float32)
    return buffer.at[clipped].add(outbound)


def incoming(received, neighbour):
    active = (neighbour >= 0).astype(jnp.float32)
    picked = jnp.take(received, jnp.maximum(neighbour, 0), axis=0)
    return jnp.transpose(picked, (1, 0, 2)) * active[None, :, None]


def staged(
    solution,
    residual,
    direction,
    inner_old,
    interior,
    weights,
    neighbours,
    coarse_rows,
    coarse_basis_matrix,
    local_solver,
    schur_matrix,
    extension_values,
    extension_block_index,
    coarse_inverse,
):
    peer_count = lax.axis_size("sub")
    rhs_count = residual.shape[2]
    local_faces = residual.shape[3]
    neighbour = neighbours[0, 0]
    slot_count = neighbour.shape[0]
    block_size = local_faces // slot_count
    active = jnp.repeat((neighbour >= 0).astype(jnp.float32), block_size)
    current = residual[0, 0]
    weight = weights[0, 0]
    basis_rows = coarse_basis_matrix[0, 0]
    primal = coarse_rows[0, 0]
    coarse_count = coarse_inverse.shape[1]
    face_total = coarse_count // (primal.shape[0] // slot_count) * block_size
    scaled = weight[None, :] * current
    local_solve = jnp.dot(
        scaled.astype(jnp.bfloat16), local_solver[0, 0], preferred_element_type=jnp.float32
    )
    coarse_part = contract(scaled, basis_rows, 1, 1)
    columns = lax.broadcasted_iota(jnp.int32, (primal.shape[0], coarse_count), 1)
    selector = (primal[:, None] == columns).astype(jnp.float32)
    partial_sum = jnp.dot(coarse_part, selector, precision=PRECISE)
    coarse_total = lax.psum(partial_sum, ("grp", "sub"))
    own_solution = contract(coarse_inverse, coarse_total, 1, 1)
    coarse_solution = lax.all_gather(own_solution, "sub", axis=0, tiled=True)
    coarse_local = jnp.dot(selector, coarse_solution, precision=PRECISE)
    correction = contract(coarse_local, basis_rows, 0, 0)
    weighted = weight[None, :] * (local_solve + correction)
    blocks_out = weighted.reshape(rhs_count, slot_count, block_size)
    received = lax.all_to_all(
        outgoing(blocks_out, neighbour, peer_count), "sub", split_axis=0, concat_axis=0, tiled=True
    )
    precond = weighted + incoming(received, neighbour).reshape(rhs_count, local_faces)
    inner_now = lax.psum(jnp.sum(current * precond, axis=1), ("grp", "sub")) / (2.0 * face_total)
    direction_new = precond + (inner_now / inner_old)[:, None] * direction[0, 0]
    direction_half = direction_new.astype(jnp.bfloat16)
    local_image = jnp.dot(direction_half, schur_matrix[0, 0], preferred_element_type=jnp.float32)
    image_blocks = local_image.reshape(rhs_count, slot_count, block_size)
    received_image = lax.all_to_all(
        outgoing(image_blocks, neighbour, peer_count),
        "sub",
        split_axis=0,
        concat_axis=0,
        tiled=True,
    )
    image_sum = active[None, :] * (
        local_image + incoming(received_image, neighbour).reshape(rhs_count, local_faces)
    )
    curve_term = 0.5 * jnp.sum(direction_new * image_sum, axis=1)
    curvature = lax.psum(curve_term, ("grp", "sub")) / face_total
    step_size = inner_now / curvature
    solution_new = solution[0, 0] + step_size[:, None] * direction_new
    residual_new = current - step_size[:, None] * image_sum
    direction_blocks = direction_half.reshape(rhs_count, slot_count, block_size)
    picked = jnp.take(direction_blocks, extension_block_index[0, 0], axis=1)
    extended = jnp.einsum(
        "rbjk,bjkl->rbl", picked, extension_values[0, 0], preferred_element_type=jnp.float32
    )
    extended = extended.reshape(rhs_count, -1)
    interior_new = (interior[0, 0].astype(jnp.float32) + step_size[:, None] * extended).astype(
        jnp.bfloat16
    )
    return (
        solution_new[None, None],
        residual_new[None, None],
        direction_new[None, None],
        interior_new[None, None],
        inner_now,
    )


def pieces(values):
    high = values.astype(jnp.bfloat16)
    rest = values - high.astype(jnp.float32)
    middle = rest.astype(jnp.bfloat16)
    low = (rest - middle.astype(jnp.float32)).astype(jnp.bfloat16)
    return high, middle, low


def fused_kernel(
    n_grp,
    n_sub,
    face_total,
    neighbours,
    coarse_rows,
    extension_index,
    solution_in,
    residual_in,
    direction_in,
    inner_old,
    interior_in,
    weights_in,
    basis_in,
    solver_in,
    schur_in,
    extension_in,
    inverse_in,
    solution_out,
    residual_out,
    direction_out,
    interior_out,
    inner_out,
    solution_v,
    residual_v,
    direction_v,
    interior_v,
    weights_v,
    basis_v,
    solver_v,
    schur_v,
    extension_v,
    slab_v,
    inverse_v,
    half_v,
    extended_v,
    basis_send,
    basis_recv,
    slab_recv,
    packet_send,
    packet_recv,
    solve_send,
    solve_recv,
    image_send,
    image_recv,
    curve_send,
    curve_recv,
    local_sems,
    group_send_sems,
    group_recv_sems,
    all_send_sems,
    all_recv_sems,
):
    n_all = n_grp * n_sub
    me_grp = lax.axis_index("grp")
    me_sub = lax.axis_index("sub")
    me = me_grp * n_sub + me_sub
    cases = residual_v.shape[0]
    slots = neighbours.shape[2]
    primal = coarse_rows.shape[2]
    coarse = inverse_v.shape[0]

    locals_ = {}
    for spot, (name, source, target) in enumerate(
        (
            ("weights", weights_in.at[0], weights_v),
            ("residual", residual_in.at[0, 0], residual_v),
            ("basis", basis_in.at[0, 0], basis_v),
            ("slab", inverse_in, slab_v),
            ("solver", solver_in.at[0, 0], solver_v),
            ("direction", direction_in.at[0, 0], direction_v),
            ("schur", schur_in.at[0, 0], schur_v),
            ("extension", extension_in.at[0, 0], extension_v),
            ("solution", solution_in.at[0, 0], solution_v),
            ("interior", interior_in.at[0, 0], interior_v),
        )
    ):
        locals_[name] = pltpu.make_async_copy(source, target, local_sems.at[spot])
    for copy in locals_.values():
        copy.start()

    barrier = pltpu.get_barrier_semaphore()

    def greet(off, carry):
        peer = lax.rem(me + off, n_all)
        pl.semaphore_signal(
            barrier, inc=1, device_id=(peer // n_sub, lax.rem(peer, n_sub)), device_id_type=MESH
        )
        return carry

    lax.fori_loop(1, n_all, greet, 0)

    def group_copy(kind, off, source, target):
        peer = lax.rem(me_sub + off, n_sub)
        return pltpu.make_async_remote_copy(
            src_ref=source,
            dst_ref=target.at[me_sub],
            send_sem=group_send_sems.at[kind, peer],
            recv_sem=group_recv_sems.at[kind, me_sub],
            device_id=(me_grp, peer),
            device_id_type=MESH,
        )

    def group_arrival(kind, off, source, target):
        peer = lax.rem(me_sub + off, n_sub)
        return pltpu.make_async_remote_copy(
            src_ref=source,
            dst_ref=target.at[peer],
            send_sem=group_send_sems.at[kind, peer],
            recv_sem=group_recv_sems.at[kind, peer],
            device_id=(me_grp, peer),
            device_id_type=MESH,
        )

    def all_copy(kind, off, source, target):
        peer = lax.rem(me + off, n_all)
        return pltpu.make_async_remote_copy(
            src_ref=source,
            dst_ref=target.at[me],
            send_sem=all_send_sems.at[kind, peer],
            recv_sem=all_recv_sems.at[kind, me],
            device_id=(peer // n_sub, lax.rem(peer, n_sub)),
            device_id_type=MESH,
        )

    def all_arrival(kind, off, source, target):
        peer = lax.rem(me + off, n_all)
        return pltpu.make_async_remote_copy(
            src_ref=source,
            dst_ref=target.at[peer],
            send_sem=all_send_sems.at[kind, peer],
            recv_sem=all_recv_sems.at[kind, peer],
            device_id=(peer // n_sub, lax.rem(peer, n_sub)),
            device_id_type=MESH,
        )

    def over_all(make, act, kind, source, target):
        def one(off, carry):
            act(make(kind, off, source, target))
            return carry

        lax.fori_loop(1, n_all, one, 0)

    beside = [neighbours[0, 0, k] for k in range(slots)]

    def routed(off, blocks):
        peer = lax.rem(me_sub + off, n_sub)
        total = None
        for k in range(slots):
            term = jnp.where(beside[k] == peer, blocks[k], 0.0)
            total = term if total is None else total + term
        return total

    def partner(received, k):
        block = received[jnp.maximum(beside[k], 0)]
        return jnp.where(beside[k] >= 0, block, 0.0)

    def cut(values):
        return [values[:, k * LANES : (k + 1) * LANES] for k in range(slots)]

    lane = lax.broadcasted_iota(jnp.int32, (1, LANES), 1)
    rows = jnp.full((1, LANES), -1.0, jnp.float32)
    for m in range(primal):
        rows = jnp.where(
            lax.rem(lane, FIELD) == m, coarse_rows[0, 0, m].astype(jnp.float32), rows
        )
    locals_["weights"].wait()
    locals_["residual"].wait()
    locals_["basis"].wait()
    weight = weights_v[...]
    residual = residual_v[...]
    scaled = weight * residual
    basis = jnp.concatenate(
        [basis_v[...], jnp.zeros((FIELD - primal, basis_v.shape[1]), jnp.float32)], axis=0
    )
    weighted_basis = weight * basis
    sub_field = lax.broadcasted_iota(jnp.int32, (FIELD, LANES), 0)
    basis_blocks = [jnp.where(sub_field == primal, rows, block) for block in cut(weighted_basis)]
    for off in range(1, n_sub):
        basis_send[off] = routed(off, basis_blocks)
    locals_["slab"].wait()
    slab_recv[me_sub] = slab_v[...]

    pl.semaphore_wait(barrier, n_all - 1)
    for off in range(1, n_sub):
        group_copy(0, off, basis_send.at[off], basis_recv).start()
        group_copy(1, off, slab_v, slab_recv).start()

    locals_["solver"].wait()
    solve = jnp.dot(
        scaled.astype(jnp.bfloat16), solver_v[...], preferred_element_type=jnp.float32
    )
    wide_basis = jnp.concatenate([basis] * (LANES // FIELD), axis=0)
    part = contract(scaled, wide_basis, 1, 1)
    own_dot = jnp.sum(scaled * solve, axis=1, keepdims=True)
    wide_lane = lax.broadcasted_iota(jnp.int32, (cases, LANES), 1)
    wide_case = lax.broadcasted_iota(jnp.int32, (cases, LANES), 0)
    part = jnp.where(lax.rem(wide_lane, FIELD) == primal, own_dot, part)
    part = jnp.where(wide_lane // FIELD == lax.rem(wide_case, SUBLANES), part, 0.0)
    halves = cases // SUBLANES
    packet = jnp.concatenate(
        [
            jnp.sum(part[a * SUBLANES : (a + 1) * SUBLANES], axis=0, keepdims=True)
            for a in range(halves)
        ]
        + [rows, jnp.zeros((1, LANES), jnp.float32)],
        axis=0,
    )
    packet_send[...] = packet
    packet_recv[me] = packet
    over_all(all_copy, lambda copy: copy.start(), 0, packet_send, packet_recv)
    weighted_solve = cut(weight * solve)
    for off in range(1, n_sub):
        solve_send[off] = routed(off, weighted_solve)
        group_copy(2, off, solve_send.at[off], solve_recv).start()

    coarse_id = lax.broadcasted_iota(jnp.int32, (coarse, LANES), 0).astype(jnp.float32)

    def spread(names, values):
        chosen = jnp.where(coarse_id == names, 1.0, 0.0)[:, :FIELD].astype(jnp.bfloat16)
        count = values.shape[1]
        wide = jnp.dot(
            chosen,
            jnp.concatenate(pieces(values), axis=1),
            preferred_element_type=jnp.float32,
        )
        return (wide[:, 2 * count :] + wide[:, count : 2 * count]) + wide[:, :count]

    own_spread = cut(spread(rows, weighted_basis))
    for off in range(1, n_sub):
        group_arrival(0, off, basis_send.at[off], basis_recv).wait_recv()
    spreads = []
    for k in range(slots):
        block = partner(basis_recv, k)
        names = block[primal : primal + 1]
        clean = jnp.where(sub_field == primal, 0.0, block)
        spreads.append(own_spread[k] + spread(names, clean))
    whole_spread = jnp.concatenate(spreads, axis=1)
    for off in range(1, n_sub):
        group_arrival(1, off, slab_v, slab_recv).wait_recv()
    inverse_v[...] = jnp.zeros_like(inverse_v)
    slab_rows, slab_columns = slab_v.shape
    for p in range(n_sub):
        inverse_v[p * slab_rows : (p + 1) * slab_rows, :slab_columns] = slab_recv[p]
    inverse = inverse_v[...]

    over_all(all_arrival, lambda copy: copy.wait_recv(), 0, packet_send, packet_recv)
    fields = LANES // FIELD
    tile_lane = lax.broadcasted_iota(jnp.int32, (SUBLANES, LANES), 1) // FIELD
    tile_sub = lax.broadcasted_iota(jnp.int32, (SUBLANES, LANES), 0)
    turned = [[] for _ in range(halves)]
    names = []
    for j in range(n_all // fields):
        tile = packet_recv[j * fields : (j + 1) * fields]
        for a in range(halves):
            source = tile[:, a, :]
            result = source
            for turn in range(1, fields):
                moved = pltpu.roll(
                    pltpu.roll(source, turn * FIELD, 1), SUBLANES - turn, 0
                )
                hit = lax.rem(tile_lane - tile_sub + fields, fields) == turn
                result = jnp.where(hit, moved, result)
            turned[a].append(result)
        names.append(
            jnp.sum(
                jnp.where(tile_lane == tile_sub, tile[:, halves, :], 0.0), axis=0, keepdims=True
            )
        )
    parts = jnp.concatenate(
        [jnp.concatenate(turned[a], axis=1) for a in range(halves)], axis=0
    )
    all_names = jnp.concatenate(names, axis=1)
    width = parts.shape[1]
    row_id = lax.broadcasted_iota(jnp.int32, (coarse, width), 0).astype(jnp.float32)
    selector = jnp.where(row_id == all_names, 1.0, 0.0).astype(jnp.bfloat16)
    summed = lax.dot_general(
        jnp.concatenate(pieces(parts), axis=0),
        selector,
        (((1,), (1,)), ((), ())),
        preferred_element_type=jnp.float32,
    )
    coarse_total = (summed[2 * cases :] + summed[cases : 2 * cases]) + summed[:cases]
    coarse_solution = contract(coarse_total, inverse, 1, 0)
    correction = cut(contract(coarse_solution, whole_spread, 1, 0))
    part_lane = lax.broadcasted_iota(jnp.int32, (cases, width), 1)
    dots = jnp.sum(
        jnp.where(lax.rem(part_lane, FIELD) == primal, parts, 0.0), axis=1, keepdims=True
    )
    dots = dots + jnp.sum(coarse_total * coarse_solution, axis=1, keepdims=True)
    inner = dots / face_total
    case_row = lax.broadcasted_iota(jnp.int32, (cases, cases), 0)
    case_lane = lax.broadcasted_iota(jnp.int32, (cases, cases), 1)
    inner_out[...] = jnp.sum(jnp.where(case_row == case_lane, inner, 0.0), axis=0, keepdims=True)
    old = jnp.sum(
        jnp.where(case_row == case_lane, inner_old[...], 0.0), axis=1, keepdims=True
    )
    ratio = inner / old
    for off in range(1, n_sub):
        group_arrival(2, off, solve_send.at[off], solve_recv).wait_recv()
    locals_["direction"].wait()
    news = []
    for k in range(slots):
        precond = (weighted_solve[k] + partner(solve_recv, k)) + correction[k]
        news.append(precond + ratio * direction_v[:, k * LANES : (k + 1) * LANES])
    direction_new = jnp.concatenate(news, axis=1)
    direction_half = direction_new.astype(jnp.bfloat16)
    locals_["schur"].wait()
    local_image = cut(
        jnp.dot(direction_half, schur_v[...], preferred_element_type=jnp.float32)
    )
    for off in range(1, n_sub):
        image_send[off] = routed(off, local_image)
        group_copy(3, off, image_send.at[off], image_recv).start()
    bent = None
    for k in range(slots):
        term = jnp.where(beside[k] >= 0, news[k] * local_image[k], 0.0)
        bent = term if bent is None else bent + term
    bent = jnp.sum(bent, axis=1, keepdims=True)
    bent_row = jnp.sum(jnp.where(wide_lane == wide_case, bent, 0.0), axis=0, keepdims=True)
    curve_send[...] = bent_row
    curve_recv[me] = bent_row
    over_all(all_copy, lambda copy: copy.start(), 1, curve_send, curve_recv)

    direction_out[0, 0] = direction_new
    for k in range(slots):
        half_v[k] = direction_half[:, k * LANES : (k + 1) * LANES]
    locals_["extension"].wait()
    for b in range(extension_v.shape[0]):
        total = None
        for j in range(extension_v.shape[1]):
            term = jnp.dot(
                half_v[extension_index[0, 0, b, j]],
                extension_v[b, j],
                preferred_element_type=jnp.float32,
            )
            total = term if total is None else total + term
        extended_v[:, b * LANES : (b + 1) * LANES] = total
    locals_["solution"].wait()
    locals_["interior"].wait()

    over_all(all_arrival, lambda copy: copy.wait_recv(), 1, curve_send, curve_recv)
    gathered = [curve_recv[d] for d in range(n_all)]
    while len(gathered) > 1:
        gathered = [
            sum(gathered[i + 1 : i + 2], gathered[i]) for i in range(0, len(gathered), 2)
        ]
    curvature = (
        jnp.sum(jnp.where(wide_lane == wide_case, gathered[0], 0.0), axis=1, keepdims=True)
        / face_total
    )
    step = inner / curvature
    solution_out[0, 0] = solution_v[...] + step * direction_new
    interior_out[0, 0] = (
        interior_v[...].astype(jnp.float32) + step * extended_v[...]
    ).astype(jnp.bfloat16)
    for off in range(1, n_sub):
        group_arrival(3, off, image_send.at[off], image_recv).wait_recv()
    for k in range(slots):
        image = jnp.where(beside[k] >= 0, local_image[k] + partner(image_recv, k), 0.0)
        span = slice(k * LANES, (k + 1) * LANES)
        residual_out[0, 0, :, span] = residual[:, span] - step * image

    for off in range(1, n_sub):
        group_copy(0, off, basis_send.at[off], basis_recv).wait_send()
        group_copy(1, off, slab_v, slab_recv).wait_send()
        group_copy(2, off, solve_send.at[off], solve_recv).wait_send()
        group_copy(3, off, image_send.at[off], image_recv).wait_send()
    over_all(all_copy, lambda copy: copy.wait_send(), 0, packet_send, packet_recv)
    over_all(all_copy, lambda copy: copy.wait_send(), 1, curve_send, curve_recv)


def fused(
    solution,
    residual,
    direction,
    inner_old,
    interior,
    weights,
    neighbours,
    coarse_rows,
    coarse_basis_matrix,
    local_solver,
    schur_matrix,
    extension_values,
    extension_block_index,
    coarse_inverse,
):
    n_grp, n_sub = lax.axis_size("grp"), lax.axis_size("sub")
    n_all = n_grp * n_sub
    cases, faces = residual.shape[2:]
    interior_faces = interior.shape[3]
    slots = neighbours.shape[2]
    primal = coarse_rows.shape[2]
    slab_rows, coarse_count = coarse_inverse.shape
    coarse = -(-coarse_count // LANES) * LANES
    face_total = coarse_count // (primal // slots) * (faces // slots)
    f32, bf16 = jnp.float32, jnp.bfloat16
    smem = pl.BlockSpec(memory_space=pltpu.SMEM)
    vmem = pl.BlockSpec(memory_space=pltpu.VMEM)
    far = pl.BlockSpec(memory_space=pl.ANY)
    outs = pl.pallas_call(
        functools.partial(fused_kernel, n_grp, n_sub, float(face_total)),
        out_shape=[
            jax.ShapeDtypeStruct(solution.shape, f32),
            jax.ShapeDtypeStruct(residual.shape, f32),
            jax.ShapeDtypeStruct(direction.shape, f32),
            jax.ShapeDtypeStruct(interior.shape, bf16),
            jax.ShapeDtypeStruct((1, cases), f32),
        ],
        in_specs=[smem, smem, smem, far, far, far, vmem, far, far, far, far, far, far, far],
        out_specs=[vmem] * 5,
        scratch_shapes=[
            pltpu.VMEM((cases, faces), f32),
            pltpu.VMEM((cases, faces), f32),
            pltpu.VMEM((cases, faces), f32),
            pltpu.VMEM((cases, interior_faces), bf16),
            pltpu.VMEM((1, faces), f32),
            pltpu.VMEM((primal, faces), f32),
            pltpu.VMEM((faces, faces), bf16),
            pltpu.VMEM((faces, faces), bf16),
            pltpu.VMEM(extension_values.shape[2:], bf16),
            pltpu.VMEM((slab_rows, coarse_count), f32),
            pltpu.VMEM((coarse, coarse), f32),
            pltpu.VMEM((slots, cases, LANES), bf16),
            pltpu.VMEM((cases, interior_faces), f32),
            pltpu.VMEM((n_sub, FIELD, LANES), f32),
            pltpu.VMEM((n_sub, FIELD, LANES), f32),
            pltpu.VMEM((n_sub, slab_rows, coarse_count), f32),
            pltpu.VMEM((cases // SUBLANES + 2, LANES), f32),
            pltpu.VMEM((n_all, cases // SUBLANES + 2, LANES), f32),
            pltpu.VMEM((n_sub, cases, LANES), f32),
            pltpu.VMEM((n_sub, cases, LANES), f32),
            pltpu.VMEM((n_sub, cases, LANES), f32),
            pltpu.VMEM((n_sub, cases, LANES), f32),
            pltpu.VMEM((1, LANES), f32),
            pltpu.VMEM((n_all, 1, LANES), f32),
            pltpu.SemaphoreType.DMA((10,)),
            pltpu.SemaphoreType.DMA((4, n_sub)),
            pltpu.SemaphoreType.DMA((4, n_sub)),
            pltpu.SemaphoreType.DMA((2, n_all)),
            pltpu.SemaphoreType.DMA((2, n_all)),
        ],
        compiler_params=pltpu.CompilerParams(
            collective_id=0, has_side_effects=True, vmem_limit_bytes=24 * 1024 * 1024
        ),
    )(
        neighbours,
        coarse_rows,
        extension_block_index,
        solution,
        residual,
        direction,
        inner_old.reshape(1, cases),
        interior,
        weights,
        coarse_basis_matrix,
        local_solver,
        schur_matrix,
        extension_values,
        coarse_inverse,
    )
    return (*outs[:4], outs[4].reshape(cases))


def per_device(*arrays):
    if arrays[-1].shape[1] <= COARSE_LIMIT:
        return fused(*arrays)
    return staged(*arrays)


def solution(mesh):
    in_specs = (
        P("grp", "sub", None, None),
        P("grp", "sub", None, None),
        P("grp", "sub", None, None),
        P(),
        P("grp", "sub", None, None),
        P("grp", "sub", None),
        P("grp", "sub", None),
        P("grp", "sub", None),
        P("grp", "sub", None, None),
        P("grp", "sub", None, None),
        P("grp", "sub", None, None),
        P("grp", "sub", None, None, None, None),
        P("grp", "sub", None, None),
        P("sub", None),
    )
    out_specs = (
        P("grp", "sub", None, None),
        P("grp", "sub", None, None),
        P("grp", "sub", None, None),
        P("grp", "sub", None, None),
        P(),
    )
    return jax.shard_map(
        per_device, mesh=mesh, in_specs=in_specs, out_specs=out_specs, check_vma=False
    )
```

```python
import functools

import jax
import jax.numpy as jnp
from jax import lax
from jax.experimental import pallas as pl
from jax.experimental.pallas import tpu as pltpu
from jax.sharding import PartitionSpec as P

MESH = pl.DeviceIdType.MESH
LANES = 128
SUBLANES = 8
FIELD = 16
COARSE_LIMIT = 128
HELD_BYTES = 60 * 1024 * 1024

PRECISE = lax.Precision.HIGHEST


def contract(former, latter, former_dim, latter_dim):
    return lax.dot_general(
        former, latter, (((former_dim,), (latter_dim,)), ((), ())), precision=PRECISE
    )


def outgoing(blocks, neighbour, peer_count):
    active = (neighbour >= 0).astype(jnp.float32)
    clipped = jnp.maximum(neighbour, 0)
    outbound = jnp.transpose(blocks * active[None, :, None], (1, 0, 2))
    buffer = jnp.zeros((peer_count, blocks.shape[0], blocks.shape[2]), jnp.float32)
    return buffer.at[clipped].add(outbound)


def incoming(received, neighbour):
    active = (neighbour >= 0).astype(jnp.float32)
    picked = jnp.take(received, jnp.maximum(neighbour, 0), axis=0)
    return jnp.transpose(picked, (1, 0, 2)) * active[None, :, None]


def staged(
    solution,
    residual,
    direction,
    inner_old,
    interior,
    weights,
    neighbours,
    coarse_rows,
    coarse_basis_matrix,
    local_solver,
    schur_matrix,
    extension_values,
    extension_block_index,
    coarse_inverse,
):
    peer_count = lax.axis_size("sub")
    rhs_count = residual.shape[2]
    local_faces = residual.shape[3]
    neighbour = neighbours[0, 0]
    slot_count = neighbour.shape[0]
    block_size = local_faces // slot_count
    active = jnp.repeat((neighbour >= 0).astype(jnp.float32), block_size)
    current = residual[0, 0]
    weight = weights[0, 0]
    basis_rows = coarse_basis_matrix[0, 0]
    primal = coarse_rows[0, 0]
    coarse_count = coarse_inverse.shape[1]
    face_total = coarse_count // (primal.shape[0] // slot_count) * block_size
    scaled = weight[None, :] * current
    local_solve = jnp.dot(
        scaled.astype(jnp.bfloat16), local_solver[0, 0], preferred_element_type=jnp.float32
    )
    coarse_part = contract(scaled, basis_rows, 1, 1)
    columns = lax.broadcasted_iota(jnp.int32, (primal.shape[0], coarse_count), 1)
    selector = (primal[:, None] == columns).astype(jnp.float32)
    partial_sum = jnp.dot(coarse_part, selector, precision=PRECISE)
    coarse_total = lax.psum(partial_sum, ("grp", "sub"))
    own_solution = contract(coarse_inverse, coarse_total, 1, 1)
    coarse_solution = lax.all_gather(own_solution, "sub", axis=0, tiled=True)
    coarse_local = jnp.dot(selector, coarse_solution, precision=PRECISE)
    correction = contract(coarse_local, basis_rows, 0, 0)
    weighted = weight[None, :] * (local_solve + correction)
    blocks_out = weighted.reshape(rhs_count, slot_count, block_size)
    received = lax.all_to_all(
        outgoing(blocks_out, neighbour, peer_count), "sub", split_axis=0, concat_axis=0, tiled=True
    )
    precond = weighted + incoming(received, neighbour).reshape(rhs_count, local_faces)
    inner_now = lax.psum(jnp.sum(current * precond, axis=1), ("grp", "sub")) / (2.0 * face_total)
    direction_new = precond + (inner_now / inner_old)[:, None] * direction[0, 0]
    direction_half = direction_new.astype(jnp.bfloat16)
    local_image = jnp.dot(direction_half, schur_matrix[0, 0], preferred_element_type=jnp.float32)
    image_blocks = local_image.reshape(rhs_count, slot_count, block_size)
    received_image = lax.all_to_all(
        outgoing(image_blocks, neighbour, peer_count),
        "sub",
        split_axis=0,
        concat_axis=0,
        tiled=True,
    )
    image_sum = active[None, :] * (
        local_image + incoming(received_image, neighbour).reshape(rhs_count, local_faces)
    )
    curve_term = 0.5 * jnp.sum(direction_new * image_sum, axis=1)
    curvature = lax.psum(curve_term, ("grp", "sub")) / face_total
    step_size = inner_now / curvature
    solution_new = solution[0, 0] + step_size[:, None] * direction_new
    residual_new = current - step_size[:, None] * image_sum
    direction_blocks = direction_half.reshape(rhs_count, slot_count, block_size)
    picked = jnp.take(direction_blocks, extension_block_index[0, 0], axis=1)
    extended = jnp.einsum(
        "rbjk,bjkl->rbl", picked, extension_values[0, 0], preferred_element_type=jnp.float32
    )
    extended = extended.reshape(rhs_count, -1)
    interior_new = (interior[0, 0].astype(jnp.float32) + step_size[:, None] * extended).astype(
        jnp.bfloat16
    )
    return (
        solution_new[None, None],
        residual_new[None, None],
        direction_new[None, None],
        interior_new[None, None],
        inner_now,
    )


def pieces(values):
    high = values.astype(jnp.bfloat16)
    rest = values - high.astype(jnp.float32)
    middle = rest.astype(jnp.bfloat16)
    low = (rest - middle.astype(jnp.float32)).astype(jnp.bfloat16)
    return high, middle, low


def fused_kernel(
    n_grp,
    n_sub,
    face_total,
    neighbours_in,
    rows_in,
    index_in,
    solution_in,
    residual_in,
    direction_in,
    inner_in,
    interior_in,
    weights_in,
    basis_in,
    solver_in,
    schur_in,
    extension_in,
    inverse_in,
    solution_out,
    residual_out,
    direction_out,
    interior_out,
    inner_out,
    neighbours,
    coarse_rows,
    extension_index,
    inner_old,
    split_v,
    solution_v,
    residual_v,
    direction_v,
    interior_v,
    weights_v,
    basis_v,
    solver_v,
    schur_v,
    extension_v,
    slab_v,
    inverse_v,
    half_v,
    extended_v,
    basis_send,
    basis_recv,
    slab_recv,
    packet_send,
    packet_recv,
    solve_send,
    solve_recv,
    image_send,
    image_recv,
    curve_send,
    curve_recv,
    local_sems,
    send_sems,
    recv_sems,
):
    n_all = n_grp * n_sub
    me_grp = lax.axis_index("grp")
    me_sub = lax.axis_index("sub")
    me = me_grp * n_sub + me_sub
    cases = residual_v.shape[0]
    slots = neighbours.shape[2]
    primal = coarse_rows.shape[2]
    coarse = inverse_v.shape[0]

    locals_ = {}
    for spot, (name, source, target) in enumerate(
        (
            ("neighbours", neighbours_in, neighbours),
            ("rows", rows_in, coarse_rows),
            ("weights", weights_in.at[0], weights_v),
            ("residual", residual_in.at[0, 0], residual_v),
            ("basis", basis_in.at[0], basis_v),
            ("slab", inverse_in, slab_v),
            ("solver", solver_in.at[0, 0], solver_v),
            ("inner", inner_in, inner_old),
            ("index", index_in, extension_index),
            ("direction", direction_in.at[0, 0], direction_v),
            ("schur", schur_in.at[0, 0], schur_v),
            ("extension", extension_in.at[0, 0], extension_v),
            ("solution", solution_in.at[0, 0], solution_v),
            ("interior", interior_in.at[0, 0], interior_v),
        )
    ):
        locals_[name] = pltpu.make_async_copy(source, target, local_sems.at[spot])
    for copy in locals_.values():
        copy.start()

    barrier = pltpu.get_barrier_semaphore()

    sub_peers = [lax.rem(me_sub + off, n_sub) for off in range(n_sub)]
    grp_peers = [lax.rem(me_grp + off, n_grp) for off in range(n_grp)]
    everyone = [(g, s) for s in sub_peers for g in grp_peers][1:]
    for peer in everyone:
        pl.semaphore_signal(barrier, inc=1, device_id=peer, device_id_type=MESH)

    def group_copy(kind, off, source, target):
        return pltpu.make_async_remote_copy(
            src_ref=source,
            dst_ref=target.at[me_sub],
            send_sem=send_sems.at[kind],
            recv_sem=recv_sems.at[kind],
            device_id=(me_grp, sub_peers[off]),
            device_id_type=MESH,
        )

    def all_copy(kind, peer, source, target):
        return pltpu.make_async_remote_copy(
            src_ref=source,
            dst_ref=target.at[me],
            send_sem=send_sems.at[kind],
            recv_sem=recv_sems.at[kind],
            device_id=peer,
            device_id_type=MESH,
        )

    def all_of(kind, target):
        span = target.at[pl.ds(0, target.shape[0] - 1)]
        return pltpu.make_async_remote_copy(
            src_ref=span,
            dst_ref=span,
            send_sem=send_sems.at[kind],
            recv_sem=recv_sems.at[kind],
            device_id=everyone[0],
            device_id_type=MESH,
        )

    locals_["neighbours"].wait()
    locals_["rows"].wait()
    beside = [neighbours[0, 0, k] for k in range(slots)]

    def routed(off, blocks):
        peer = sub_peers[off]
        total = None
        for k in range(slots):
            term = jnp.where(beside[k] == peer, blocks[k], 0.0)
            total = term if total is None else total + term
        return total

    def partner(received, k):
        block = received[jnp.maximum(beside[k], 0)]
        return jnp.where(beside[k] >= 0, block, 0.0)

    def cut(values):
        return [values[:, k * LANES : (k + 1) * LANES] for k in range(slots)]

    lane = lax.broadcasted_iota(jnp.int32, (1, LANES), 1)
    rows = jnp.full((1, LANES), -1.0, jnp.float32)
    for m in range(primal):
        rows = jnp.where(
            lax.rem(lane, FIELD) == m, coarse_rows[0, 0, m].astype(jnp.float32), rows
        )
    locals_["weights"].wait()
    locals_["residual"].wait()
    locals_["basis"].wait()
    weight = weights_v[...]
    residual = residual_v[...]
    scaled = weight * residual
    basis = jnp.concatenate(
        [basis_v[m] for m in range(primal)]
        + [jnp.zeros((FIELD - primal, basis_v.shape[2]), jnp.float32)],
        axis=0,
    )
    weighted_basis = weight * basis
    sub_field = lax.broadcasted_iota(jnp.int32, (FIELD, LANES), 0)
    basis_blocks = [jnp.where(sub_field == primal, rows, block) for block in cut(weighted_basis)]
    for off in range(1, n_sub):
        basis_send[off] = routed(off, basis_blocks)
    wide_lane = lax.broadcasted_iota(jnp.int32, (cases, LANES), 1)
    wide_case = lax.broadcasted_iota(jnp.int32, (cases, LANES), 0)
    part = jnp.zeros((cases, LANES), jnp.float32)
    for m in range(primal):
        column = jnp.sum(scaled * basis[m : m + 1], axis=1, keepdims=True)
        part = jnp.where(lax.rem(wide_lane, FIELD) == m, column, part)
    locals_["slab"].wait()
    slab_recv[me_sub] = slab_v[...]

    pl.semaphore_wait(barrier, n_all - 1)
    for off in range(1, n_sub):
        group_copy(0, off, basis_send.at[off], basis_recv).start()
        group_copy(1, off, slab_v, slab_recv).start()

    locals_["solver"].wait()
    solve = jnp.dot(
        scaled.astype(jnp.bfloat16), solver_v[...], preferred_element_type=jnp.float32
    )
    own_dot = jnp.sum(scaled * solve, axis=1, keepdims=True)
    part = jnp.where(lax.rem(wide_lane, FIELD) == primal, own_dot, part)
    part = jnp.where(wide_lane // FIELD == lax.rem(wide_case, SUBLANES), part, 0.0)
    halves = cases // SUBLANES
    packet = jnp.concatenate(
        [
            jnp.sum(part[a * SUBLANES : (a + 1) * SUBLANES], axis=0, keepdims=True)
            for a in range(halves)
        ]
        + [rows, jnp.zeros((1, LANES), jnp.float32)],
        axis=0,
    )
    packet_send[...] = packet
    packet_recv[me] = packet
    for peer in everyone:
        all_copy(4, peer, packet_send, packet_recv).start()
    weighted_solve = cut(weight * solve)
    for off in range(1, n_sub):
        solve_send[off] = routed(off, weighted_solve)
        group_copy(2, off, solve_send.at[off], solve_recv).start()

    coarse_id = lax.broadcasted_iota(jnp.int32, (coarse, LANES), 0).astype(jnp.float32)

    def spread(names, values):
        chosen = jnp.where(coarse_id == names, 1.0, 0.0)[:, :FIELD].astype(jnp.bfloat16)
        count = values.shape[1]
        wide = jnp.dot(
            chosen,
            jnp.concatenate(pieces(values), axis=1),
            preferred_element_type=jnp.float32,
        )
        return (wide[:, 2 * count :] + wide[:, count : 2 * count]) + wide[:, :count]

    own_spread = cut(spread(rows, weighted_basis))
    all_of(0, basis_recv).wait_recv()
    spreads = []
    for k in range(slots):
        block = partner(basis_recv, k)
        names = block[primal : primal + 1]
        clean = jnp.where(sub_field == primal, 0.0, block)
        spreads.append(own_spread[k] + spread(names, clean))
    whole_spread = jnp.concatenate(spreads, axis=1)
    all_of(1, slab_recv).wait_recv()
    inverse_v[...] = jnp.zeros_like(inverse_v)
    slab_rows, slab_columns = slab_v.shape
    for p in range(n_sub):
        inverse_v[p * slab_rows : (p + 1) * slab_rows, :slab_columns] = slab_recv[p]
    inverse = inverse_v[...]
    both = jnp.concatenate([inverse, contract(inverse, whole_spread, 1, 0)], axis=1)
    split_v[0], split_v[1] = pieces(both)[:2]

    all_of(4, packet_recv).wait_recv()
    fields = LANES // FIELD
    tile_lane = lax.broadcasted_iota(jnp.int32, (SUBLANES, LANES), 1) // FIELD
    tile_sub = lax.broadcasted_iota(jnp.int32, (SUBLANES, LANES), 0)
    turned = [[] for _ in range(halves)]
    names = []
    for j in range(n_all // fields):
        tile = packet_recv[j * fields : (j + 1) * fields]
        for a in range(halves):
            source = tile[:, a, :]
            result = source
            for turn in range(1, fields):
                moved = pltpu.roll(
                    pltpu.roll(source, turn * FIELD, 1), SUBLANES - turn, 0
                )
                hit = lax.rem(tile_lane - tile_sub + fields, fields) == turn
                result = jnp.where(hit, moved, result)
            turned[a].append(result)
        names.append(
            jnp.sum(
                jnp.where(tile_lane == tile_sub, tile[:, halves, :], 0.0), axis=0, keepdims=True
            )
        )
    parts = jnp.concatenate(
        [jnp.concatenate(turned[a], axis=1) for a in range(halves)], axis=0
    )
    all_names = jnp.concatenate(names, axis=1)
    width = parts.shape[1]
    row_id = lax.broadcasted_iota(jnp.int32, (coarse, width), 0).astype(jnp.float32)
    selector = jnp.where(row_id == all_names, 1.0, 0.0).astype(jnp.bfloat16)
    summed = lax.dot_general(
        jnp.concatenate(pieces(parts), axis=0),
        selector,
        (((1,), (1,)), ((), ())),
        preferred_element_type=jnp.float32,
    )
    coarse_total = (summed[2 * cases :] + summed[cases : 2 * cases]) + summed[:cases]
    stacked = jnp.concatenate(pieces(coarse_total)[:2], axis=0)
    solved = jnp.dot(stacked, split_v[0], preferred_element_type=jnp.float32) + jnp.dot(
        stacked, split_v[1], preferred_element_type=jnp.float32
    )
    solved = solved[:cases] + solved[cases:]
    coarse_solution = solved[:, :coarse]
    correction = cut(solved[:, coarse:])
    part_lane = lax.broadcasted_iota(jnp.int32, (cases, width), 1)
    dots = jnp.sum(
        jnp.where(lax.rem(part_lane, FIELD) == primal, parts, 0.0), axis=1, keepdims=True
    )
    dots = dots + jnp.sum(coarse_total * coarse_solution, axis=1, keepdims=True)
    inner = dots / face_total
    case_row = lax.broadcasted_iota(jnp.int32, (cases, cases), 0)
    case_lane = lax.broadcasted_iota(jnp.int32, (cases, cases), 1)
    inner_out[...] = jnp.sum(jnp.where(case_row == case_lane, inner, 0.0), axis=0, keepdims=True)
    locals_["inner"].wait()
    old = jnp.sum(
        jnp.where(case_row == case_lane, inner_old[...], 0.0), axis=1, keepdims=True
    )
    ratio = inner / old
    all_of(2, solve_recv).wait_recv()
    locals_["direction"].wait()
    news = []
    for k in range(slots):
        precond = (weighted_solve[k] + partner(solve_recv, k)) + correction[k]
        news.append(precond + ratio * direction_v[:, k * LANES : (k + 1) * LANES])
    direction_new = jnp.concatenate(news, axis=1)
    direction_half = direction_new.astype(jnp.bfloat16)
    locals_["schur"].wait()
    local_image = cut(
        jnp.dot(direction_half, schur_v[...], preferred_element_type=jnp.float32)
    )
    for off in range(1, n_sub):
        image_send[off] = routed(off, local_image)
        group_copy(3, off, image_send.at[off], image_recv).start()
    bent = None
    for k in range(slots):
        term = jnp.where(beside[k] >= 0, news[k] * local_image[k], 0.0)
        bent = term if bent is None else bent + term
    bent = jnp.sum(bent, axis=1, keepdims=True)
    bent_row = jnp.sum(jnp.where(wide_lane == wide_case, bent, 0.0), axis=0, keepdims=True)
    curve_send[...] = bent_row
    curve_recv[me] = bent_row
    for peer in everyone:
        all_copy(5, peer, curve_send, curve_recv).start()

    direction_out[0, 0] = direction_new
    for k in range(slots):
        half_v[k] = direction_half[:, k * LANES : (k + 1) * LANES]
    locals_["index"].wait()
    locals_["extension"].wait()
    for b in range(extension_v.shape[0]):
        total = None
        for j in range(extension_v.shape[1]):
            term = jnp.dot(
                half_v[extension_index[0, 0, j, b]],
                extension_v[b, j],
                preferred_element_type=jnp.float32,
            )
            total = term if total is None else total + term
        extended_v[:, b * LANES : (b + 1) * LANES] = total
    locals_["solution"].wait()
    locals_["interior"].wait()

    all_of(5, curve_recv).wait_recv()
    gathered = [curve_recv[d] for d in range(n_all)]
    while len(gathered) > 1:
        gathered = [
            sum(gathered[i + 1 : i + 2], gathered[i]) for i in range(0, len(gathered), 2)
        ]
    curvature = (
        jnp.sum(jnp.where(wide_lane == wide_case, gathered[0], 0.0), axis=1, keepdims=True)
        / face_total
    )
    step = inner / curvature
    solution_out[0, 0] = solution_v[...] + step * direction_new
    interior_out[0, 0] = (
        interior_v[...].astype(jnp.float32) + step * extended_v[...]
    ).astype(jnp.bfloat16)
    all_of(3, image_recv).wait_recv()
    for k in range(slots):
        image = jnp.where(beside[k] >= 0, local_image[k] + partner(image_recv, k), 0.0)
        span = slice(k * LANES, (k + 1) * LANES)
        residual_out[0, 0, :, span] = residual[:, span] - step * image

    for kind, target in enumerate(
        (basis_recv, slab_recv, solve_recv, image_recv, packet_recv, curve_recv)
    ):
        all_of(kind, target).wait_send()


def handed_kernel(count, *refs):
    for i in range(count):
        refs[count + i][...] = refs[i][...]


def fused(
    solution,
    residual,
    direction,
    inner_old,
    interior,
    weights,
    neighbours,
    coarse_rows,
    coarse_basis_matrix,
    local_solver,
    schur_matrix,
    extension_values,
    extension_block_index,
    coarse_inverse,
):
    n_grp, n_sub = lax.axis_size("grp"), lax.axis_size("sub")
    n_all = n_grp * n_sub
    cases, faces = residual.shape[2:]
    interior_faces = interior.shape[3]
    slots = neighbours.shape[2]
    primal = coarse_rows.shape[2]
    slab_rows, coarse_count = coarse_inverse.shape
    coarse = -(-coarse_count // LANES) * LANES
    face_total = coarse_count // (primal // slots) * (faces // slots)
    f32, bf16 = jnp.float32, jnp.bfloat16
    vmem = pl.BlockSpec(memory_space=pltpu.VMEM)
    far = pl.BlockSpec(memory_space=pltpu.HBM)
    outs = pl.pallas_call(
        functools.partial(fused_kernel, n_grp, n_sub, float(face_total)),
        out_shape=[
            jax.ShapeDtypeStruct(solution.shape, f32),
            jax.ShapeDtypeStruct(residual.shape, f32),
            jax.ShapeDtypeStruct(direction.shape, f32),
            jax.ShapeDtypeStruct(interior.shape, bf16),
            jax.ShapeDtypeStruct((1, cases), f32),
        ],
        in_specs=[far] * 14,
        out_specs=[vmem] * 5,
        scratch_shapes=[
            pltpu.SMEM(neighbours.shape, jnp.int32),
            pltpu.SMEM(coarse_rows.shape, jnp.int32),
            pltpu.SMEM((1, 1) + extension_block_index.shape[:1:-1], jnp.int32),
            pltpu.VMEM((1, cases), f32),
            pltpu.VMEM((2, coarse, coarse + faces), bf16),
            pltpu.VMEM((cases, faces), f32),
            pltpu.VMEM((cases, faces), f32),
            pltpu.VMEM((cases, faces), f32),
            pltpu.VMEM((cases, interior_faces), bf16),
            pltpu.VMEM((1, faces), f32),
            pltpu.VMEM((primal, 1, faces), f32),
            pltpu.VMEM((faces, faces), bf16),
            pltpu.VMEM((faces, faces), bf16),
            pltpu.VMEM(extension_values.shape[2:], bf16),
            pltpu.VMEM((slab_rows, coarse_count), f32),
            pltpu.VMEM((coarse, coarse), f32),
            pltpu.VMEM((slots, cases, LANES), bf16),
            pltpu.VMEM((cases, interior_faces), f32),
            pltpu.VMEM((n_sub, FIELD, LANES), f32),
            pltpu.VMEM((n_sub, FIELD, LANES), f32),
            pltpu.VMEM((n_sub, slab_rows, coarse_count), f32),
            pltpu.VMEM((cases // SUBLANES + 2, LANES), f32),
            pltpu.VMEM((n_all, cases // SUBLANES + 2, LANES), f32),
            pltpu.VMEM((n_sub, cases, LANES), f32),
            pltpu.VMEM((n_sub, cases, LANES), f32),
            pltpu.VMEM((n_sub, cases, LANES), f32),
            pltpu.VMEM((n_sub, cases, LANES), f32),
            pltpu.VMEM((1, LANES), f32),
            pltpu.VMEM((n_all, 1, LANES), f32),
            pltpu.SemaphoreType.DMA((14,)),
            pltpu.SemaphoreType.DMA((6,)),
            pltpu.SemaphoreType.DMA((6,)),
        ],
        compiler_params=pltpu.CompilerParams(
            collective_id=0, has_side_effects=True, vmem_limit_bytes=HELD_BYTES
        ),
    )(
        neighbours,
        coarse_rows,
        jnp.swapaxes(extension_block_index, 2, 3),
        solution,
        residual,
        direction,
        inner_old.reshape(1, cases),
        interior,
        weights,
        jnp.swapaxes(coarse_basis_matrix, 1, 2),
        local_solver,
        schur_matrix,
        extension_values,
        coarse_inverse,
    )
    handed = pl.pallas_call(
        functools.partial(handed_kernel, len(outs)),
        out_shape=[jax.ShapeDtypeStruct(out.shape, out.dtype) for out in outs],
        in_specs=[vmem] * len(outs),
        out_specs=[vmem] * len(outs),
        compiler_params=pltpu.CompilerParams(vmem_limit_bytes=HELD_BYTES),
    )(*outs)
    return (*handed[:4], handed[4].reshape(cases))


def per_device(*arrays):
    if arrays[-1].shape[1] <= COARSE_LIMIT:
        return fused(*arrays)
    return staged(*arrays)


def solution(mesh):
    in_specs = (
        P("grp", "sub", None, None),
        P("grp", "sub", None, None),
        P("grp", "sub", None, None),
        P(),
        P("grp", "sub", None, None),
        P("grp", "sub", None),
        P("grp", "sub", None),
        P("grp", "sub", None),
        P("grp", "sub", None, None),
        P("grp", "sub", None, None),
        P("grp", "sub", None, None),
        P("grp", "sub", None, None, None, None),
        P("grp", "sub", None, None),
        P("sub", None),
    )
    out_specs = (
        P("grp", "sub", None, None),
        P("grp", "sub", None, None),
        P("grp", "sub", None, None),
        P("grp", "sub", None, None),
        P(),
    )
    return jax.shard_map(
        per_device, mesh=mesh, in_specs=in_specs, out_specs=out_specs, check_vma=False
    )
```

```python
import functools

import jax
import jax.numpy as jnp
from jax import lax
from jax.experimental import pallas as pl
from jax.experimental.pallas import tpu as pltpu
from jax.sharding import PartitionSpec as P

MESH = pl.DeviceIdType.MESH
LANES = 128
SUBLANES = 8
FIELD = 16
COARSE_LIMIT = 128
HELD_BYTES = 60 * 1024 * 1024

PRECISE = lax.Precision.HIGHEST


def contract(former, latter, former_dim, latter_dim):
    return lax.dot_general(
        former, latter, (((former_dim,), (latter_dim,)), ((), ())), precision=PRECISE
    )


def outgoing(blocks, neighbour, peer_count):
    active = (neighbour >= 0).astype(jnp.float32)
    clipped = jnp.maximum(neighbour, 0)
    outbound = jnp.transpose(blocks * active[None, :, None], (1, 0, 2))
    buffer = jnp.zeros((peer_count, blocks.shape[0], blocks.shape[2]), jnp.float32)
    return buffer.at[clipped].add(outbound)


def incoming(received, neighbour):
    active = (neighbour >= 0).astype(jnp.float32)
    picked = jnp.take(received, jnp.maximum(neighbour, 0), axis=0)
    return jnp.transpose(picked, (1, 0, 2)) * active[None, :, None]


def staged(
    solution,
    residual,
    direction,
    inner_old,
    interior,
    weights,
    neighbours,
    coarse_rows,
    coarse_basis_matrix,
    local_solver,
    schur_matrix,
    extension_values,
    extension_block_index,
    coarse_inverse,
):
    peer_count = lax.axis_size("sub")
    rhs_count = residual.shape[2]
    local_faces = residual.shape[3]
    neighbour = neighbours[0, 0]
    slot_count = neighbour.shape[0]
    block_size = local_faces // slot_count
    active = jnp.repeat((neighbour >= 0).astype(jnp.float32), block_size)
    current = residual[0, 0]
    weight = weights[0, 0]
    basis_rows = coarse_basis_matrix[0, 0]
    primal = coarse_rows[0, 0]
    coarse_count = coarse_inverse.shape[1]
    face_total = coarse_count // (primal.shape[0] // slot_count) * block_size
    scaled = weight[None, :] * current
    local_solve = jnp.dot(
        scaled.astype(jnp.bfloat16), local_solver[0, 0], preferred_element_type=jnp.float32
    )
    coarse_part = contract(scaled, basis_rows, 1, 1)
    columns = lax.broadcasted_iota(jnp.int32, (primal.shape[0], coarse_count), 1)
    selector = (primal[:, None] == columns).astype(jnp.float32)
    partial_sum = jnp.dot(coarse_part, selector, precision=PRECISE)
    coarse_total = lax.psum(partial_sum, ("grp", "sub"))
    own_solution = contract(coarse_inverse, coarse_total, 1, 1)
    coarse_solution = lax.all_gather(own_solution, "sub", axis=0, tiled=True)
    coarse_local = jnp.dot(selector, coarse_solution, precision=PRECISE)
    correction = contract(coarse_local, basis_rows, 0, 0)
    weighted = weight[None, :] * (local_solve + correction)
    blocks_out = weighted.reshape(rhs_count, slot_count, block_size)
    received = lax.all_to_all(
        outgoing(blocks_out, neighbour, peer_count), "sub", split_axis=0, concat_axis=0, tiled=True
    )
    precond = weighted + incoming(received, neighbour).reshape(rhs_count, local_faces)
    inner_now = lax.psum(jnp.sum(current * precond, axis=1), ("grp", "sub")) / (2.0 * face_total)
    direction_new = precond + (inner_now / inner_old)[:, None] * direction[0, 0]
    direction_half = direction_new.astype(jnp.bfloat16)
    local_image = jnp.dot(direction_half, schur_matrix[0, 0], preferred_element_type=jnp.float32)
    image_blocks = local_image.reshape(rhs_count, slot_count, block_size)
    received_image = lax.all_to_all(
        outgoing(image_blocks, neighbour, peer_count),
        "sub",
        split_axis=0,
        concat_axis=0,
        tiled=True,
    )
    image_sum = active[None, :] * (
        local_image + incoming(received_image, neighbour).reshape(rhs_count, local_faces)
    )
    curve_term = 0.5 * jnp.sum(direction_new * image_sum, axis=1)
    curvature = lax.psum(curve_term, ("grp", "sub")) / face_total
    step_size = inner_now / curvature
    solution_new = solution[0, 0] + step_size[:, None] * direction_new
    residual_new = current - step_size[:, None] * image_sum
    direction_blocks = direction_half.reshape(rhs_count, slot_count, block_size)
    picked = jnp.take(direction_blocks, extension_block_index[0, 0], axis=1)
    extended = jnp.einsum(
        "rbjk,bjkl->rbl", picked, extension_values[0, 0], preferred_element_type=jnp.float32
    )
    extended = extended.reshape(rhs_count, -1)
    interior_new = (interior[0, 0].astype(jnp.float32) + step_size[:, None] * extended).astype(
        jnp.bfloat16
    )
    return (
        solution_new[None, None],
        residual_new[None, None],
        direction_new[None, None],
        interior_new[None, None],
        inner_now,
    )


def pieces(values):
    high = values.astype(jnp.bfloat16)
    rest = values - high.astype(jnp.float32)
    middle = rest.astype(jnp.bfloat16)
    low = (rest - middle.astype(jnp.float32)).astype(jnp.bfloat16)
    return high, middle, low


def fused_kernel(
    n_grp,
    n_sub,
    face_total,
    neighbours_in,
    rows_in,
    index_in,
    solution_in,
    residual_in,
    direction_in,
    inner_in,
    interior_in,
    weights_in,
    basis_in,
    solver_in,
    schur_in,
    extension_in,
    inverse_in,
    solution_out,
    residual_out,
    direction_out,
    interior_out,
    inner_out,
    neighbours,
    coarse_rows,
    extension_index,
    inner_old,
    split_v,
    solution_v,
    residual_v,
    direction_v,
    interior_v,
    weights_v,
    basis_v,
    solver_v,
    schur_v,
    extension_v,
    slab_v,
    inverse_v,
    half_v,
    extended_v,
    basis_send,
    basis_recv,
    slab_recv,
    packet_send,
    packet_recv,
    solve_send,
    solve_recv,
    image_send,
    image_recv,
    curve_send,
    curve_recv,
    local_sems,
    send_sems,
    recv_sems,
):
    n_all = n_grp * n_sub
    me_grp = lax.axis_index("grp")
    me_sub = lax.axis_index("sub")
    me = me_grp * n_sub + me_sub
    cases = residual_v.shape[0]
    slots = neighbours.shape[2]
    primal = coarse_rows.shape[2]
    coarse = inverse_v.shape[0]

    locals_ = {}
    for spot, (name, source, target) in enumerate(
        (
            ("neighbours", neighbours_in, neighbours),
            ("rows", rows_in, coarse_rows),
            ("weights", weights_in.at[0], weights_v),
            ("residual", residual_in.at[0, 0], residual_v),
            ("basis", basis_in.at[0], basis_v),
            ("slab", inverse_in, slab_v),
            ("solver", solver_in.at[0, 0], solver_v),
            ("inner", inner_in, inner_old),
            ("index", index_in, extension_index),
            ("direction", direction_in.at[0, 0], direction_v),
            ("schur", schur_in.at[0, 0], schur_v),
            ("extension", extension_in.at[0, 0], extension_v),
            ("solution", solution_in.at[0, 0], solution_v),
            ("interior", interior_in.at[0, 0], interior_v),
        )
    ):
        locals_[name] = pltpu.make_async_copy(source, target, local_sems.at[spot])
    for copy in locals_.values():
        copy.start()

    barrier = pltpu.get_barrier_semaphore()

    sub_peers = [lax.rem(me_sub + off, n_sub) for off in range(n_sub)]
    grp_peers = [lax.rem(me_grp + off, n_grp) for off in range(n_grp)]
    everyone = [(g, s) for s in sub_peers for g in grp_peers][1:]
    for peer in everyone:
        pl.semaphore_signal(barrier, inc=1, device_id=peer, device_id_type=MESH)

    def group_copy(kind, off, source, target):
        return pltpu.make_async_remote_copy(
            src_ref=source,
            dst_ref=target.at[me_sub],
            send_sem=send_sems.at[kind],
            recv_sem=recv_sems.at[kind],
            device_id=(me_grp, sub_peers[off]),
            device_id_type=MESH,
        )

    def all_copy(kind, peer, source, target):
        return pltpu.make_async_remote_copy(
            src_ref=source,
            dst_ref=target.at[me],
            send_sem=send_sems.at[kind],
            recv_sem=recv_sems.at[kind],
            device_id=peer,
            device_id_type=MESH,
        )

    def all_of(kind, target):
        span = target.at[pl.ds(0, target.shape[0] - 1)]
        return pltpu.make_async_remote_copy(
            src_ref=span,
            dst_ref=span,
            send_sem=send_sems.at[kind],
            recv_sem=recv_sems.at[kind],
            device_id=everyone[0],
            device_id_type=MESH,
        )

    locals_["neighbours"].wait()
    locals_["rows"].wait()
    beside = [neighbours[0, 0, k] for k in range(slots)]

    def routed(off, blocks):
        peer = sub_peers[off]
        total = None
        for k in range(slots):
            term = jnp.where(beside[k] == peer, blocks[k], 0.0)
            total = term if total is None else total + term
        return total

    def partner(received, k):
        block = received[jnp.maximum(beside[k], 0)]
        return jnp.where(beside[k] >= 0, block, 0.0)

    def cut(values):
        return [values[:, k * LANES : (k + 1) * LANES] for k in range(slots)]

    lane = lax.broadcasted_iota(jnp.int32, (1, LANES), 1)
    rows = jnp.full((1, LANES), -1.0, jnp.float32)
    for m in range(primal):
        rows = jnp.where(
            lax.rem(lane, FIELD) == m, coarse_rows[0, 0, m].astype(jnp.float32), rows
        )
    locals_["weights"].wait()
    locals_["residual"].wait()
    locals_["basis"].wait()
    weight = weights_v[...]
    residual = residual_v[...]
    scaled = weight * residual
    basis = jnp.concatenate(
        [basis_v[m] for m in range(primal)]
        + [jnp.zeros((FIELD - primal, basis_v.shape[2]), jnp.float32)],
        axis=0,
    )
    weighted_basis = weight * basis
    sub_field = lax.broadcasted_iota(jnp.int32, (FIELD, LANES), 0)
    basis_blocks = [jnp.where(sub_field == primal, rows, block) for block in cut(weighted_basis)]
    for off in range(1, n_sub):
        basis_send[off] = routed(off, basis_blocks)
    wide_lane = lax.broadcasted_iota(jnp.int32, (cases, LANES), 1)
    wide_case = lax.broadcasted_iota(jnp.int32, (cases, LANES), 0)
    part = jnp.zeros((cases, LANES), jnp.float32)
    for m in range(primal):
        column = jnp.sum(scaled * basis[m : m + 1], axis=1, keepdims=True)
        part = jnp.where(lax.rem(wide_lane, FIELD) == m, column, part)
    locals_["slab"].wait()
    slab_recv[me_sub] = slab_v[...]

    locals_["solver"].wait()
    solve = jnp.dot(
        scaled.astype(jnp.bfloat16), solver_v[...], preferred_element_type=jnp.float32
    )
    own_dot = jnp.sum(scaled * solve, axis=1, keepdims=True)
    part = jnp.where(lax.rem(wide_lane, FIELD) == primal, own_dot, part)
    part = jnp.where(wide_lane // FIELD == lax.rem(wide_case, SUBLANES), part, 0.0)
    halves = cases // SUBLANES
    packet = jnp.concatenate(
        [
            jnp.sum(part[a * SUBLANES : (a + 1) * SUBLANES], axis=0, keepdims=True)
            for a in range(halves)
        ]
        + [rows, jnp.zeros((1, LANES), jnp.float32)],
        axis=0,
    )
    packet_send[...] = packet
    packet_recv[me] = packet
    pl.semaphore_wait(barrier, n_all - 1)
    for peer in everyone:
        all_copy(4, peer, packet_send, packet_recv).start()
    for off in range(1, n_sub):
        group_copy(0, off, basis_send.at[off], basis_recv).start()
        group_copy(1, off, slab_v, slab_recv).start()
    weighted_solve = cut(weight * solve)
    for off in range(1, n_sub):
        solve_send[off] = routed(off, weighted_solve)
        group_copy(2, off, solve_send.at[off], solve_recv).start()

    coarse_id = lax.broadcasted_iota(jnp.int32, (coarse, LANES), 0).astype(jnp.float32)

    def spread(names, values):
        chosen = jnp.where(coarse_id == names, 1.0, 0.0)[:, :FIELD].astype(jnp.bfloat16)
        count = values.shape[1]
        wide = jnp.dot(
            chosen,
            jnp.concatenate(pieces(values), axis=1),
            preferred_element_type=jnp.float32,
        )
        return (wide[:, 2 * count :] + wide[:, count : 2 * count]) + wide[:, :count]

    own_spread = cut(spread(rows, weighted_basis))
    all_of(0, basis_recv).wait_recv()
    spreads = []
    for k in range(slots):
        block = partner(basis_recv, k)
        names = block[primal : primal + 1]
        clean = jnp.where(sub_field == primal, 0.0, block)
        spreads.append(own_spread[k] + spread(names, clean))
    whole_spread = jnp.concatenate(spreads, axis=1)
    all_of(1, slab_recv).wait_recv()
    inverse_v[...] = jnp.zeros_like(inverse_v)
    slab_rows, slab_columns = slab_v.shape
    for p in range(n_sub):
        inverse_v[p * slab_rows : (p + 1) * slab_rows, :slab_columns] = slab_recv[p]
    inverse = inverse_v[...]
    both = jnp.concatenate([inverse, contract(inverse, whole_spread, 1, 0)], axis=1)
    split_v[0], split_v[1] = pieces(both)[:2]

    all_of(4, packet_recv).wait_recv()
    fields = LANES // FIELD
    tile_lane = lax.broadcasted_iota(jnp.int32, (SUBLANES, LANES), 1) // FIELD
    tile_sub = lax.broadcasted_iota(jnp.int32, (SUBLANES, LANES), 0)
    turned = [[] for _ in range(halves)]
    names = []
    for j in range(n_all // fields):
        tile = packet_recv[j * fields : (j + 1) * fields]
        for a in range(halves):
            source = tile[:, a, :]
            result = source
            for turn in range(1, fields):
                moved = pltpu.roll(
                    pltpu.roll(source, turn * FIELD, 1), SUBLANES - turn, 0
                )
                hit = lax.rem(tile_lane - tile_sub + fields, fields) == turn
                result = jnp.where(hit, moved, result)
            turned[a].append(result)
        names.append(
            jnp.sum(
                jnp.where(tile_lane == tile_sub, tile[:, halves, :], 0.0), axis=0, keepdims=True
            )
        )
    parts = jnp.concatenate(
        [jnp.concatenate(turned[a], axis=1) for a in range(halves)], axis=0
    )
    all_names = jnp.concatenate(names, axis=1)
    width = parts.shape[1]
    row_id = lax.broadcasted_iota(jnp.int32, (coarse, width), 0).astype(jnp.float32)
    selector = jnp.where(row_id == all_names, 1.0, 0.0).astype(jnp.bfloat16)
    summed = lax.dot_general(
        jnp.concatenate(pieces(parts), axis=0),
        selector,
        (((1,), (1,)), ((), ())),
        preferred_element_type=jnp.float32,
    )
    coarse_total = (summed[2 * cases :] + summed[cases : 2 * cases]) + summed[:cases]
    stacked = jnp.concatenate(pieces(coarse_total)[:2], axis=0)
    solved = jnp.dot(stacked, split_v[0], preferred_element_type=jnp.float32) + jnp.dot(
        stacked, split_v[1], preferred_element_type=jnp.float32
    )
    solved = solved[:cases] + solved[cases:]
    coarse_solution = solved[:, :coarse]
    correction = cut(solved[:, coarse:])
    part_lane = lax.broadcasted_iota(jnp.int32, (cases, width), 1)
    dots = jnp.sum(
        jnp.where(lax.rem(part_lane, FIELD) == primal, parts, 0.0), axis=1, keepdims=True
    )
    dots = dots + jnp.sum(coarse_total * coarse_solution, axis=1, keepdims=True)
    inner = dots / face_total
    case_row = lax.broadcasted_iota(jnp.int32, (cases, cases), 0)
    case_lane = lax.broadcasted_iota(jnp.int32, (cases, cases), 1)
    inner_out[...] = jnp.sum(jnp.where(case_row == case_lane, inner, 0.0), axis=0, keepdims=True)
    locals_["inner"].wait()
    old = jnp.sum(
        jnp.where(case_row == case_lane, inner_old[...], 0.0), axis=1, keepdims=True
    )
    ratio = inner / old
    all_of(2, solve_recv).wait_recv()
    locals_["direction"].wait()
    news = []
    for k in range(slots):
        precond = (weighted_solve[k] + partner(solve_recv, k)) + correction[k]
        news.append(precond + ratio * direction_v[:, k * LANES : (k + 1) * LANES])
    direction_new = jnp.concatenate(news, axis=1)
    direction_half = direction_new.astype(jnp.bfloat16)
    locals_["schur"].wait()
    local_image = cut(
        jnp.dot(direction_half, schur_v[...], preferred_element_type=jnp.float32)
    )
    bent = None
    for k in range(slots):
        term = jnp.where(beside[k] >= 0, news[k] * local_image[k], 0.0)
        bent = term if bent is None else bent + term
    bent = jnp.sum(bent, axis=1, keepdims=True)
    bent_row = jnp.sum(jnp.where(wide_lane == wide_case, bent, 0.0), axis=0, keepdims=True)
    curve_send[...] = bent_row
    curve_recv[me] = bent_row
    for peer in everyone:
        all_copy(5, peer, curve_send, curve_recv).start()
    for off in range(1, n_sub):
        image_send[off] = routed(off, local_image)
        group_copy(3, off, image_send.at[off], image_recv).start()

    direction_out[0, 0] = direction_new
    for k in range(slots):
        half_v[k] = direction_half[:, k * LANES : (k + 1) * LANES]
    locals_["index"].wait()
    locals_["extension"].wait()
    for b in range(extension_v.shape[0]):
        total = None
        for j in range(extension_v.shape[1]):
            term = jnp.dot(
                half_v[extension_index[0, 0, j, b]],
                extension_v[b, j],
                preferred_element_type=jnp.float32,
            )
            total = term if total is None else total + term
        extended_v[:, b * LANES : (b + 1) * LANES] = total
    locals_["solution"].wait()
    locals_["interior"].wait()

    all_of(5, curve_recv).wait_recv()
    gathered = [curve_recv[d] for d in range(n_all)]
    while len(gathered) > 1:
        gathered = [
            sum(gathered[i + 1 : i + 2], gathered[i]) for i in range(0, len(gathered), 2)
        ]
    curvature = (
        jnp.sum(jnp.where(wide_lane == wide_case, gathered[0], 0.0), axis=1, keepdims=True)
        / face_total
    )
    step = inner / curvature
    solution_out[0, 0] = solution_v[...] + step * direction_new
    interior_out[0, 0] = (
        interior_v[...].astype(jnp.float32) + step * extended_v[...]
    ).astype(jnp.bfloat16)
    all_of(3, image_recv).wait_recv()
    for k in range(slots):
        image = jnp.where(beside[k] >= 0, local_image[k] + partner(image_recv, k), 0.0)
        span = slice(k * LANES, (k + 1) * LANES)
        residual_out[0, 0, :, span] = residual[:, span] - step * image

    for kind, target in enumerate(
        (basis_recv, slab_recv, solve_recv, image_recv, packet_recv, curve_recv)
    ):
        all_of(kind, target).wait_send()


def handed_kernel(count, *refs):
    for i in range(count):
        refs[count + i][...] = refs[i][...]


def fused(
    solution,
    residual,
    direction,
    inner_old,
    interior,
    weights,
    neighbours,
    coarse_rows,
    coarse_basis_matrix,
    local_solver,
    schur_matrix,
    extension_values,
    extension_block_index,
    coarse_inverse,
):
    n_grp, n_sub = lax.axis_size("grp"), lax.axis_size("sub")
    n_all = n_grp * n_sub
    cases, faces = residual.shape[2:]
    interior_faces = interior.shape[3]
    slots = neighbours.shape[2]
    primal = coarse_rows.shape[2]
    slab_rows, coarse_count = coarse_inverse.shape
    coarse = -(-coarse_count // LANES) * LANES
    face_total = coarse_count // (primal // slots) * (faces // slots)
    f32, bf16 = jnp.float32, jnp.bfloat16
    vmem = pl.BlockSpec(memory_space=pltpu.VMEM)
    far = pl.BlockSpec(memory_space=pltpu.HBM)
    outs = pl.pallas_call(
        functools.partial(fused_kernel, n_grp, n_sub, float(face_total)),
        out_shape=[
            jax.ShapeDtypeStruct(solution.shape, f32),
            jax.ShapeDtypeStruct(residual.shape, f32),
            jax.ShapeDtypeStruct(direction.shape, f32),
            jax.ShapeDtypeStruct(interior.shape, bf16),
            jax.ShapeDtypeStruct((1, cases), f32),
        ],
        in_specs=[far] * 14,
        out_specs=[vmem] * 5,
        scratch_shapes=[
            pltpu.SMEM(neighbours.shape, jnp.int32),
            pltpu.SMEM(coarse_rows.shape, jnp.int32),
            pltpu.SMEM((1, 1) + extension_block_index.shape[:1:-1], jnp.int32),
            pltpu.VMEM((1, cases), f32),
            pltpu.VMEM((2, coarse, coarse + faces), bf16),
            pltpu.VMEM((cases, faces), f32),
            pltpu.VMEM((cases, faces), f32),
            pltpu.VMEM((cases, faces), f32),
            pltpu.VMEM((cases, interior_faces), bf16),
            pltpu.VMEM((1, faces), f32),
            pltpu.VMEM((primal, 1, faces), f32),
            pltpu.VMEM((faces, faces), bf16),
            pltpu.VMEM((faces, faces), bf16),
            pltpu.VMEM(extension_values.shape[2:], bf16),
            pltpu.VMEM((slab_rows, coarse_count), f32),
            pltpu.VMEM((coarse, coarse), f32),
            pltpu.VMEM((slots, cases, LANES), bf16),
            pltpu.VMEM((cases, interior_faces), f32),
            pltpu.VMEM((n_sub, FIELD, LANES), f32),
            pltpu.VMEM((n_sub, FIELD, LANES), f32),
            pltpu.VMEM((n_sub, slab_rows, coarse_count), f32),
            pltpu.VMEM((cases // SUBLANES + 2, LANES), f32),
            pltpu.VMEM((n_all, cases // SUBLANES + 2, LANES), f32),
            pltpu.VMEM((n_sub, cases, LANES), f32),
            pltpu.VMEM((n_sub, cases, LANES), f32),
            pltpu.VMEM((n_sub, cases, LANES), f32),
            pltpu.VMEM((n_sub, cases, LANES), f32),
            pltpu.VMEM((1, LANES), f32),
            pltpu.VMEM((n_all, 1, LANES), f32),
            pltpu.SemaphoreType.DMA((14,)),
            pltpu.SemaphoreType.DMA((6,)),
            pltpu.SemaphoreType.DMA((6,)),
        ],
        compiler_params=pltpu.CompilerParams(
            collective_id=0, has_side_effects=True, vmem_limit_bytes=HELD_BYTES
        ),
    )(
        neighbours,
        coarse_rows,
        jnp.swapaxes(extension_block_index, 2, 3),
        solution,
        residual,
        direction,
        inner_old.reshape(1, cases),
        interior,
        weights,
        jnp.swapaxes(coarse_basis_matrix, 1, 2),
        local_solver,
        schur_matrix,
        extension_values,
        coarse_inverse,
    )
    handed = pl.pallas_call(
        functools.partial(handed_kernel, len(outs)),
        out_shape=[jax.ShapeDtypeStruct(out.shape, out.dtype) for out in outs],
        in_specs=[vmem] * len(outs),
        out_specs=[vmem] * len(outs),
        compiler_params=pltpu.CompilerParams(vmem_limit_bytes=HELD_BYTES),
    )(*outs)
    return (*handed[:4], handed[4].reshape(cases))


def per_device(*arrays):
    if arrays[-1].shape[1] <= COARSE_LIMIT:
        return fused(*arrays)
    return staged(*arrays)


def solution(mesh):
    in_specs = (
        P("grp", "sub", None, None),
        P("grp", "sub", None, None),
        P("grp", "sub", None, None),
        P(),
        P("grp", "sub", None, None),
        P("grp", "sub", None),
        P("grp", "sub", None),
        P("grp", "sub", None),
        P("grp", "sub", None, None),
        P("grp", "sub", None, None),
        P("grp", "sub", None, None),
        P("grp", "sub", None, None, None, None),
        P("grp", "sub", None, None),
        P("sub", None),
    )
    out_specs = (
        P("grp", "sub", None, None),
        P("grp", "sub", None, None),
        P("grp", "sub", None, None),
        P("grp", "sub", None, None),
        P(),
    )
    return jax.shard_map(
        per_device, mesh=mesh, in_specs=in_specs, out_specs=out_specs, check_vma=False
    )
```
